512 devices in a mesh: tm: 128 (over y, z, x_hi), space: 4 (over x_lo, core).
Axes of the slice: x: 4 (x_hi: 2, x_lo: 2; x = x_hi * 2 + x_lo), y: 4, z: 16, core: 2. Of those that a mesh axis runs over, the one named last changes fastest.
Arguments:
- right_side: float32 [128, 128, 2048], P('tm', 'space'), may hold values from -24 to 24
- iterate: float32 [128, 128, 2048], P('tm', 'space'), may hold values from -6 to 6
- diffusion: float32 [128, 2048], P('space'), may hold values from 0.1 to 1
- wind_rows: float32 [128, 2048], P('space'), may hold values from -0.2 to 0.2
- wind_cols: float32 [128, 2048], P('space'), may hold values from -0.2 to 0.2
Outputs:
- updated: float32 [128, 128, 2048], P('tm', 'space')
The draws below stay inside these ranges and needn't reach their ends.
All inputs are finite; a program needn't handle non-finite values.
Results may differ from the reference program's by a relative error of at most 0.0003.
Values sent between devices are 32-bit elements; how exact they have to be, the bound alone decides.
A program may use at most 64 MiB of HBM per device.

```python
import math
import jax
import jax.numpy as jnp

NX = 2048
SWEEPS = 4
STEPS = 128
NY = 128


def block_scale(stream_key, extent, split, least, high):
    level, own = 1.0, jax.random.fold_in(stream_key, 6)
    for position, blocks in split:
        draws = jnp.exp(jax.random.uniform(jax.random.fold_in(own, position), (blocks,), jnp.float32, least / len(split), high / len(split)))
        level = level * jnp.repeat(draws, extent[position] // blocks).reshape([-1 if axis == position else 1 for axis in range(len(extent))])
    return level


def centred(own_key, extent, spread, bound, shards=(), dtype=jnp.bfloat16):
    loudness = block_scale(own_key, extent, shards, -0.22, 0.18) if shards else 1.0
    values = jax.random.normal(own_key, extent, jnp.float32) * spread * loudness
    return jnp.minimum(jnp.maximum(values, -bound), bound).astype(dtype)


def setup_inputs(seed: int = 0) -> dict:
    keys = jax.random.split(jax.random.key(seed), 6)
    right_side = centred(keys[0], (STEPS, NY, NX), 4.0, 24.0, ((0, 128), (1, 4)), jnp.float32)
    iterate = centred(keys[1], (STEPS, NY, NX), 1.0, 6.0, ((0, 128), (1, 4)), jnp.float32)
    diffusion = jnp.clip(jnp.exp(math.log(1.0) - 2.3025851 * jax.random.uniform(keys[2], (NY, NX), jnp.float32) ** block_scale(keys[2], (NY, NX), ((0, 4),), -0.2, 0.2)), 0.1, 1.0)
    wind_rows = jnp.clip(jax.random.uniform(keys[3], (NY, NX), jnp.float32, -0.2, 0.2) * block_scale(keys[3], (NY, NX), ((0, 4),), -0.4, 0.0), -0.2, 0.2)
    wind_cols = jnp.clip(jax.random.uniform(keys[4], (NY, NX), jnp.float32, -0.2, 0.2) * block_scale(keys[4], (NY, NX), ((0, 4),), -0.4, 0.0), -0.2, 0.2)
    return dict(right_side=right_side, iterate=iterate, diffusion=diffusion, wind_rows=wind_rows, wind_cols=wind_cols)


ALPHA = 0.1
RELAX_WEIGHTS = (0.7, 0.9, 0.8, 1.0)


def operate(grid_field, diffusion, wind_rows, wind_cols):
    padded = jnp.pad(grid_field, ((0, 0), (1, 1), (1, 1)))
    row_next = padded[:, 2:, 1:-1]
    row_prior = padded[:, :-2, 1:-1]
    col_next = padded[:, 1:-1, 2:]
    col_prior = padded[:, 1:-1, :-2]
    return grid_field + diffusion * (4.0 * grid_field - row_next - row_prior - col_next - col_prior) + 0.5 * wind_rows * (row_next - row_prior) + 0.5 * wind_cols * (col_next - col_prior)


def reference(right_side, iterate, diffusion, wind_rows, wind_cols):
    step_count = right_side.shape[0]
    previous = jnp.concatenate([jnp.zeros_like(iterate[:1]), iterate[:-1]], axis=0)
    residual = right_side - operate(iterate, diffusion, wind_rows, wind_cols) + previous
    time_grid = jnp.arange(step_count).astype(jnp.float32)
    log_rate = math.log(ALPHA) / step_count
    scaled = residual * jnp.exp(time_grid * log_rate)[:, None, None]
    spectrum = jnp.fft.fft(scaled, axis=0)
    source_re = jnp.real(spectrum)
    source_im = jnp.imag(spectrum)
    radius = math.exp(log_rate)
    phase_angle = (-2.0 * math.pi / step_count) * time_grid
    shift_re = (radius * jnp.cos(phase_angle))[:, None, None]
    shift_im = (radius * jnp.sin(phase_angle))[:, None, None]
    diag_re = 1.0 - shift_re + 4.0 * diffusion
    diag_im = -shift_im
    modulus = diag_re * diag_re + diag_im * diag_im
    inverse_re = diag_re / modulus
    inverse_im = -diag_im / modulus
    estimate_re = RELAX_WEIGHTS[0] * (source_re * inverse_re - source_im * inverse_im)
    estimate_im = RELAX_WEIGHTS[0] * (source_re * inverse_im + source_im * inverse_re)
    for sweep_index in range(1, SWEEPS):
        image_re = operate(estimate_re, diffusion, wind_rows, wind_cols)
        image_im = operate(estimate_im, diffusion, wind_rows, wind_cols)
        image_re = image_re - (estimate_re * shift_re - estimate_im * shift_im)
        image_im = image_im - (estimate_re * shift_im + estimate_im * shift_re)
        resid_re = source_re - image_re
        resid_im = source_im - image_im
        weight = RELAX_WEIGHTS[sweep_index]
        estimate_re = estimate_re + weight * (resid_re * inverse_re - resid_im * inverse_im)
        estimate_im = estimate_im + weight * (resid_re * inverse_im + resid_im * inverse_re)
    restored = jnp.real(jnp.fft.ifft(estimate_re + 1j * estimate_im, axis=0))
    return iterate + restored * jnp.exp(-time_grid * log_rate)[:, None, None]
```

```python
import math

import jax
import jax.numpy as jnp
import numpy as np
from jax import lax
from jax.experimental import pallas as pl
from jax.experimental.pallas import tpu as pltpu
from jax.sharding import PartitionSpec as P

MESH = pl.DeviceIdType.MESH
ALPHA = 0.1
RELAX_WEIGHTS = (0.7, 0.9, 0.8, 1.0)
T = 128
ROWS = 32
COLS = 2048
HIGHEST = lax.Precision.HIGHEST


def tables():
    n = np.arange(T)
    k = np.arange(64)
    rate = math.log(ALPHA) / T
    angle = 2.0 * math.pi * ((n[:, None] * k[None, :]) % T) / T
    forward = np.concatenate([np.cos(angle), -np.sin(angle)], axis=1)
    forward[:, 64] = np.where(n % 2 == 0, 1.0, -1.0)
    back = 2.0 * forward
    back[:, 0] *= 0.5
    back[:, 64] *= 0.5
    forward = forward * np.exp(n * rate)[:, None]
    back = back * (np.exp(-n * rate) / T)[:, None]
    radius = math.exp(rate)
    phase = 2.0 * math.pi * k / T
    shift = np.zeros((8, T))
    shift[0, :64] = radius * np.cos(phase)
    shift[0, 64:] = radius * np.cos(phase)
    shift[0, 64] = -radius
    shift[1, :64] = radius * np.sin(phase)
    shift[1, 64:] = -radius * np.sin(phase)
    shift[1, 64] = 0.0
    return [np.asarray(a, np.float32) for a in (forward, back, shift)]


def stripe_of(t):
    return lax.rem(t, 2) * 64 + lax.div(t, 32) * 16 + lax.rem(lax.div(t, 2), 16)


def holder_of(q):
    return lax.rem(lax.div(q, 16), 4) * 32 + lax.rem(q, 16) * 2 + lax.div(q, 64)


def swap_groups(v):
    row = lax.broadcasted_iota(jnp.int32, v.shape, 1)
    lane = lax.broadcasted_iota(jnp.int32, v.shape, 2)
    for m in (1, 2, 4):
        low_row = row & m == 0
        low_lane = lane & (16 * m) == 0
        up = pltpu.roll(pltpu.roll(v, 8 - m, axis=1), 16 * m, axis=2)
        down = up if m == 4 else pltpu.roll(pltpu.roll(v, m, axis=1), 128 - 16 * m, axis=2)
        v = jnp.where(low_row == low_lane, v, jnp.where(low_row, up, down))
    return v


def kernel(
    rs_ref, u_ref, d_ref, wr_ref, wc_ref, fwd_ref, back_ref, shift_ref, out_ref,
    above, below, prior, edge_top, edge_low, plain, sent, got, made, back_got, stack, turned,
    north, south, east, west, inv_a, inv_b, src, est_a, est_b, dummy,
    row_send, row_recv, prior_send, prior_recv, edge_send, edge_recv,
    halo_send, halo_recv, out_send, out_recv, own_sem, joined,
):
    t = lax.axis_index("tm")
    s = lax.axis_index("space")
    y, z, h = lax.div(t, 32), lax.rem(lax.div(t, 2), 16), lax.rem(t, 2)
    q = stripe_of(t)
    up_s, down_s = lax.rem(s + 3, 4), lax.rem(s + 1, 4)
    next_t, prior_t = lax.rem(t + 1, T), lax.rem(t + T - 1, T)
    left_t, right_t = holder_of(lax.rem(q + T - 1, T)), holder_of(lax.rem(q + 1, T))

    def peer_z(i):
        return y * 32 + lax.rem(z + i, 16) * 2 + h

    def peer_yh(i):
        g = lax.rem(y * 2 + h + i, 8)
        return lax.div(g, 2) * 32 + z * 2 + lax.rem(g, 2)

    def peer(i):
        k = lax.div(i + 1, 2)
        return lax.rem(t + lax.rem(i, 2) * 2 * k - k + T, T)

    barrier = pltpu.get_barrier_semaphore()

    def greet(semaphore, who, at):
        pl.semaphore_signal(semaphore, inc=1, device_id=(who, at), device_id_type=MESH)

    def greet_z(i, carry):
        greet(barrier, peer_z(i), s)
        return carry

    def greet_yh(i, carry):
        greet(barrier, peer_yh(i), s)
        return carry

    for at in (up_s, down_s):
        for who in (t, left_t, right_t):
            greet(barrier, who, at)
    for who in (next_t, prior_t, left_t, right_t):
        greet(barrier, who, s)
    lax.fori_loop(1, 16, greet_z, 0)
    lax.fori_loop(1, 8, greet_yh, 0)
    pl.semaphore_wait(barrier, 32)

    def remote(source, target, send, recv, who, at):
        return pltpu.make_async_remote_copy(
            src_ref=source, dst_ref=target, send_sem=send, recv_sem=recv,
            device_id=(who, at), device_id_type=MESH,
        )

    row_copies = [
        remote(u_ref.at[0, pl.ds(ROWS - 8, 8)], above, row_send.at[0], row_recv.at[0], t, down_s),
        remote(u_ref.at[0, pl.ds(0, 8)], below, row_send.at[1], row_recv.at[1], t, up_s),
    ]
    for copy in row_copies:
        copy.start()
    shift_copy = remote(u_ref.at[0], prior, prior_send, prior_recv, next_t, s)
    shift_copy.start()

    def greet_joined(i, carry):
        greet(joined, peer_yh(i), s)
        return carry

    lax.fori_loop(1, 8, greet_joined, 0)
    base = pl.multiple_of(jnp.minimum(lax.div(jnp.maximum(2 * q - 1, 0), 16), 14) * 128, 128)
    window = pl.ds(base, 256)
    edge_copies = []
    for k, ref in enumerate((d_ref, wr_ref, wc_ref)):
        edge_copies.append(
            remote(ref.at[pl.ds(ROWS - 8, 8), window], edge_top.at[k], edge_send.at[k], edge_recv.at[k], t, down_s)
        )
        edge_copies.append(
            remote(ref.at[pl.ds(0, 8), window], edge_low.at[k], edge_send.at[3 + k], edge_recv.at[3 + k], t, up_s)
        )
    for copy in edge_copies:
        copy.start()

    for copy in row_copies:
        copy.wait()
    field = u_ref[0]
    row = lax.broadcasted_iota(jnp.int32, (ROWS, COLS), 0)
    col = lax.broadcasted_iota(jnp.int32, (ROWS, COLS), 1)
    top = jnp.where(s > 0, above[7:8, :], 0.0)
    low = jnp.where(s < 3, below[0:1, :], 0.0)
    row_prior = jnp.where(row == 0, top, pltpu.roll(field, 1, axis=0))
    row_next = jnp.where(row == ROWS - 1, low, pltpu.roll(field, ROWS - 1, axis=0))
    col_prior = jnp.where(col == 0, 0.0, pltpu.roll(field, 1, axis=1))
    col_next = jnp.where(col == COLS - 1, 0.0, pltpu.roll(field, COLS - 1, axis=1))
    image = (
        field
        + d_ref[...] * (4.0 * field - row_next - row_prior - col_next - col_prior)
        + 0.5 * wr_ref[...] * (row_next - row_prior)
        + 0.5 * wc_ref[...] * (col_next - col_prior)
    )
    plain[...] = rs_ref[0] - image

    shift_copy.wait()

    def pack(cb, carry):
        lanes = pl.ds(pl.multiple_of(cb * 128, 128), 128)
        residual = plain[:, lanes] + jnp.where(t > 0, prior[:, lanes], 0.0)
        sent[:, pl.ds(pl.multiple_of(cb * 8, 8), 8), :] = swap_groups(residual.reshape(4, 8, 128))
        return carry

    lax.fori_loop(0, 16, pack, 0)
    pl.semaphore_wait(joined, 7)

    def send_stripe(i, carry):
        who = peer(i)
        remote(
            sent.at[:, pl.ds(stripe_of(who), 1), :], got.at[:, pl.ds(t, 1), :], out_send.at[0], out_recv.at[0], who, s
        ).start()
        return carry

    lax.fori_loop(1, T, send_stripe, 0)
    own = pltpu.make_async_copy(sent.at[:, pl.ds(q, 1), :], got.at[:, pl.ds(t, 1), :], own_sem)
    own.start()

    for copy in edge_copies:
        copy.wait()
    stack[...] = jnp.zeros_like(stack)
    for k, ref in enumerate((d_ref, wr_ref, wc_ref)):
        stack[pl.ds(38 * k, 3), :] = edge_top[k, 5:8, :]
        stack[pl.ds(38 * k + 3, ROWS), :] = ref[:, window]
        stack[pl.ds(38 * k + 35, 3), :] = edge_low[k, 0:3, :]
    turned[0:8, :] = jnp.zeros((8, 128), jnp.float32)
    turned[264:272, :] = jnp.zeros((8, 128), jnp.float32)
    turned[8:136, :] = stack[:, 0:128].T
    turned[136:264, :] = stack[:, 128:256].T
    offset = 16 * q - base
    left_tile = turned[pl.ds(pl.multiple_of(offset, 8), 8), :]
    middle = turned[pl.ds(pl.multiple_of(offset + 8, 8), 16), :]
    right_tile = turned[pl.ds(pl.multiple_of(offset + 24, 8), 8), :]
    tile_row = lax.broadcasted_iota(jnp.int32, (8, 128), 0)
    columns = jnp.concatenate([middle, jnp.where(tile_row < 4, right_tile, left_tile)], axis=0)
    cell = lax.broadcasted_iota(jnp.int32, (24, 128), 0)
    inside_cols = jnp.logical_and(
        jnp.logical_or(cell < 16, jnp.logical_or(cell >= 20, q < T - 1)), jnp.logical_or(cell < 20, q > 0)
    )
    shift_re = shift_ref[0:1, :]
    shift_im = shift_ref[1:2, :]

    def prepare(r, carry):
        def spread(k):
            turn = lax.rem(256 - 38 * k - r, 128)
            return jnp.broadcast_to(pltpu.roll(columns, turn, axis=1)[:, 0:1], (24, 128))

        diffusion = spread(0)
        half_rows = 0.5 * spread(1)
        half_cols = 0.5 * spread(2)
        south[r] = diffusion - half_rows
        north[r] = diffusion + half_rows
        east[r] = diffusion - half_cols
        west[r] = diffusion + half_cols
        diag = 1.0 - shift_re + 4.0 * diffusion
        modulus = 1.0 / (diag * diag + shift_im * shift_im)
        grid_row = s * ROWS + r - 3
        inside = jnp.logical_and(inside_cols, jnp.logical_and(grid_row >= 0, grid_row < 128))
        inv_a[r] = jnp.where(inside, diag * modulus, 0.0)
        inv_b[r] = jnp.where(inside, shift_im * modulus, 0.0)
        return carry

    lax.fori_loop(0, 38, prepare, 0)

    own.wait()
    arrived = remote(dummy, dummy, out_send.at[0], out_recv.at[0], next_t, s)
    arrived.wait_recv()
    for j in range(4):
        spectrum = lax.dot_general(
            got[j], fwd_ref[...], (((0,), (0,)), ((), ())), precision=HIGHEST, preferred_element_type=jnp.float32
        )
        src[pl.ds(3 + 8 * j, 8), 0:16, :] = spectrum.reshape(8, 16, 128)

    halo_copies = []
    for ds, at in ((-1, up_s), (0, s), (1, down_s)):
        from_row, to_row, rows = {-1: (3, 35, 3), 0: (3, 3, ROWS), 1: (ROWS, 0, 3)}[ds]
        for dq, who in ((-1, left_t), (0, t), (1, right_t)):
            if ds == 0 and dq == 0:
                continue
            from_col, to_col, cols = {-1: (0, 16, 4), 0: (0, 0, 16), 1: (12, 20, 4)}[dq]
            k = len(halo_copies)
            halo_copies.append(
                remote(
                    src.at[pl.ds(from_row, rows), pl.ds(from_col, cols), :],
                    src.at[pl.ds(to_row, rows), pl.ds(to_col, cols), :],
                    halo_send.at[k], halo_recv.at[k], who, at,
                )
            )
    for copy in halo_copies:
        copy.start()
    arrived.wait_send()
    for copy in halo_copies:
        copy.wait()

    def times_inverse(v, rows):
        return v * inv_a[rows] + pltpu.roll(v, 64, axis=2) * inv_b[rows]

    def first(i, carry):
        rows = pl.ds(2 * i, 2)
        est_a[rows] = RELAX_WEIGHTS[0] * times_inverse(src[rows], rows)
        return carry

    lax.fori_loop(0, 19, first, 0)

    def sweep(weight, start, count, old, new):
        def step(i, carry):
            begin = start + count * i
            rows = pl.ds(begin, count)
            here = old[rows]
            near = (
                south[rows] * old[pl.ds(begin + 1, count)]
                + north[rows] * old[pl.ds(begin - 1, count)]
                + east[rows] * pltpu.roll(here, 23, axis=1)
                + west[rows] * pltpu.roll(here, 1, axis=1)
            )
            moved = times_inverse(src[rows] + near, rows)
            new[rows] = (1.0 - weight) * here + weight * moved
            return carry

        return step

    lax.fori_loop(0, 18, sweep(RELAX_WEIGHTS[1], 1, 2, est_a, est_b), 0)
    lax.fori_loop(0, 17, sweep(RELAX_WEIGHTS[2], 2, 2, est_b, est_a), 0)
    lax.fori_loop(0, 16, sweep(RELAX_WEIGHTS[3], 3, 2, est_a, est_b), 0)

    for j in range(4):
        estimate = est_b[pl.ds(3 + 8 * j, 8), 0:16, :].reshape(128, 128)
        made[j] = lax.dot_general(
            back_ref[...], estimate, (((1,), (1,)), ((), ())), precision=HIGHEST, preferred_element_type=jnp.float32
        )

    def send_step(i, carry):
        who = peer(i)
        remote(
            made.at[:, pl.ds(who, 1), :], back_got.at[:, pl.ds(q, 1), :], out_send.at[1], out_recv.at[1], who, s
        ).start()
        return carry

    lax.fori_loop(1, T, send_step, 0)
    own_back = pltpu.make_async_copy(made.at[:, pl.ds(t, 1), :], back_got.at[:, pl.ds(q, 1), :], own_sem)
    own_back.start()
    own_back.wait()
    returned = remote(dummy, dummy, out_send.at[1], out_recv.at[1], next_t, s)
    returned.wait()

    def unpack(cb, carry):
        lanes = pl.ds(pl.multiple_of(cb * 128, 128), 128)
        restored = swap_groups(back_got[:, pl.ds(pl.multiple_of(cb * 8, 8), 8), :])
        out_ref[0, :, lanes] = u_ref[0, :, lanes] + restored.reshape(ROWS, 128)
        return carry

    lax.fori_loop(0, 16, unpack, 0)


def shards(right_side, iterate, diffusion, wind_rows, wind_cols):
    forward, back, shift = (jnp.asarray(a) for a in tables())
    vmem = pl.BlockSpec(memory_space=pltpu.VMEM)
    dma = pltpu.SemaphoreType.DMA

    def space(*shape):
        return pltpu.VMEM(shape, jnp.float32)

    scratch = [
        space(8, COLS), space(8, COLS), space(ROWS, COLS),
        space(3, 8, 256), space(3, 8, 256),
        space(ROWS, COLS), space(4, T, 128), space(4, T, 128),
        space(4, T, 128), space(4, T, 128),
        space(128, 256), space(272, 128),
    ]
    scratch += [space(38, 24, 128)] * 9
    scratch += [space(T - 1, 4, 128)]
    scratch += [
        dma((2,)), dma((2,)), dma, dma, dma((6,)), dma((6,)), dma((8,)), dma((8,)), dma((2,)), dma((2,)), dma,
        pltpu.SemaphoreType.REGULAR,
    ]
    return pl.pallas_call(
        kernel,
        out_shape=jax.ShapeDtypeStruct(iterate.shape, jnp.float32),
        in_specs=[vmem] * 8,
        out_specs=vmem,
        scratch_shapes=scratch,
        compiler_params=pltpu.CompilerParams(
            collective_id=0, has_side_effects=True, vmem_limit_bytes=48 * 1024 * 1024
        ),
        name="correction",
    )(right_side, iterate, diffusion, wind_rows, wind_cols, forward, back, shift)


def solution(mesh):
    fields = P("tm", "space", None)
    cells = P("space", None)
    return jax.shard_map(
        shards, mesh=mesh, in_specs=(fields, fields, cells, cells, cells), out_specs=fields, check_vma=False
    )
```

```python
import math

import jax
import jax.numpy as jnp
import numpy as np
from jax import lax
from jax.experimental import pallas as pl
from jax.experimental.pallas import tpu as pltpu
from jax.sharding import PartitionSpec as P

MESH = pl.DeviceIdType.MESH
ALPHA = 0.1
RELAX_WEIGHTS = (0.7, 0.9, 0.8, 1.0)
T = 128
ROWS = 32
COLS = 2048


def tables():
    n = np.arange(T)
    k = np.arange(64)
    rate = math.log(ALPHA) / T
    angle = 2.0 * math.pi * ((n[:, None] * k[None, :]) % T) / T
    forward = np.concatenate([np.cos(angle), -np.sin(angle)], axis=1)
    forward[:, 64] = np.where(n % 2 == 0, 1.0, -1.0)
    back = 2.0 * forward
    back[:, 0] *= 0.5
    back[:, 64] *= 0.5
    forward = forward * np.exp(n * rate)[:, None]
    back = back * (np.exp(-n * rate) / T)[:, None]
    radius = math.exp(rate)
    phase = 2.0 * math.pi * k / T
    shift = np.zeros((8, T))
    shift[0, :64] = radius * np.cos(phase)
    shift[0, 64:] = radius * np.cos(phase)
    shift[0, 64] = -radius
    shift[1, :64] = radius * np.sin(phase)
    shift[1, 64:] = -radius * np.sin(phase)
    shift[1, 64] = 0.0
    return [np.asarray(a, np.float32) for a in (forward, back, shift)]


def stripe_of(t):
    return lax.rem(t, 2) * 64 + lax.div(t, 32) * 16 + lax.rem(lax.div(t, 2), 16)


def holder_of(q):
    return lax.rem(lax.div(q, 16), 4) * 32 + lax.rem(q, 16) * 2 + lax.div(q, 64)


def split(v):
    high = v.astype(jnp.bfloat16)
    return high, (v - high.astype(jnp.float32)).astype(jnp.bfloat16)


def product(a, b, dims):
    terms = [
        lax.dot_general(left, right, (dims, ((), ())), preferred_element_type=jnp.float32)
        for left, right in ((a[0], b[0]), (a[0], b[1]), (a[1], b[0]))
    ]
    return terms[0] + (terms[1] + terms[2])


def swap_groups(v):
    row = lax.broadcasted_iota(jnp.int32, v.shape, 1)
    lane = lax.broadcasted_iota(jnp.int32, v.shape, 2)
    for m in (1, 2, 4):
        low_row = row & m == 0
        low_lane = lane & (16 * m) == 0
        up = pltpu.roll(pltpu.roll(v, 8 - m, axis=1), 16 * m, axis=2)
        down = up if m == 4 else pltpu.roll(pltpu.roll(v, m, axis=1), 128 - 16 * m, axis=2)
        v = jnp.where(low_row == low_lane, v, jnp.where(low_row, up, down))
    return v


def kernel(
    rs_hbm, u_hbm, d_hbm, wr_hbm, wc_hbm, fwd_hbm, back_hbm, shift_hbm, out_ref,
    rs_ref, u_ref, d_ref, wr_ref, wc_ref, fwd_ref, back_ref, shift_ref,
    above, below, prior, edge_top, edge_low, plain, sent, got, made, back_got, stack, turned,
    north, south, east, west, inv_a, inv_b, src, est_a, est_b, dummy,
    row_send, row_recv, prior_send, prior_recv, edge_send, edge_recv,
    halo_send, halo_recv, out_send, out_recv, own_sem, load_sem, joined,
):
    loads = []
    for k, (source, target) in enumerate(
        (
            (u_hbm.at[0], u_ref), (d_hbm, d_ref), (wr_hbm, wr_ref), (wc_hbm, wc_ref), (rs_hbm.at[0], rs_ref),
            (fwd_hbm, fwd_ref), (back_hbm, back_ref), (shift_hbm, shift_ref),
        )
    ):
        loads.append(pltpu.make_async_copy(source, target, load_sem.at[k]))
        loads[k].start()
    t = lax.axis_index("tm")
    s = lax.axis_index("space")
    y, z, h = lax.div(t, 32), lax.rem(lax.div(t, 2), 16), lax.rem(t, 2)
    q = stripe_of(t)
    up_s, down_s = lax.rem(s + 3, 4), lax.rem(s + 1, 4)
    next_t, prior_t = lax.rem(t + 1, T), lax.rem(t + T - 1, T)
    left_t, right_t = holder_of(lax.rem(q + T - 1, T)), holder_of(lax.rem(q + 1, T))

    def peer_z(i):
        return y * 32 + lax.rem(z + i, 16) * 2 + h

    def peer_yh(i):
        g = lax.rem(y * 2 + h + i, 8)
        return lax.div(g, 2) * 32 + z * 2 + lax.rem(g, 2)

    def far(i):
        half = lax.div(16 - i, 2)
        return lax.rem(lax.rem(15 - i, 2) * 2 * half - half + 16, 16)

    def peer(i):
        g = lax.rem(y * 2 + h + 7 - lax.rem(i, 8), 8)
        return lax.div(g, 2) * 32 + lax.rem(z + far(lax.div(i, 8)), 16) * 2 + lax.rem(g, 2)

    def part_of(who, k):
        return lax.rem(lax.div(stripe_of(who), 32) + k, 4)

    def part_lanes(who, k):
        return pl.ds(pl.multiple_of(part_of(who, k) * 512, 512), 512)

    barrier = pltpu.get_barrier_semaphore()

    def greet(semaphore, who, at):
        pl.semaphore_signal(semaphore, inc=1, device_id=(who, at), device_id_type=MESH)

    def greet_z(i, carry):
        greet(barrier, peer_z(i), s)
        return carry

    def greet_yh(i, carry):
        greet(barrier, peer_yh(i), s)
        return carry

    for at in (up_s, down_s):
        for who in (t, left_t, right_t):
            greet(barrier, who, at)
    for who in (next_t, prior_t, left_t, right_t):
        greet(barrier, who, s)
    lax.fori_loop(1, 16, greet_z, 0)
    lax.fori_loop(1, 8, greet_yh, 0)
    pl.semaphore_wait(barrier, 32)

    def remote(source, target, send, recv, who, at):
        return pltpu.make_async_remote_copy(
            src_ref=source, dst_ref=target, send_sem=send, recv_sem=recv,
            device_id=(who, at), device_id_type=MESH,
        )

    row_copies = [
        remote(u_hbm.at[0, pl.ds(ROWS - 1, 1)], above, row_send.at[0], row_recv.at[0], t, down_s),
        remote(u_hbm.at[0, pl.ds(0, 1)], below, row_send.at[1], row_recv.at[1], t, up_s),
    ]
    for copy in row_copies:
        copy.start()
    shift_copies = []
    for k in range(4):
        lanes = part_lanes(next_t, k)
        shift_copies.append(
            remote(u_hbm.at[0, :, lanes], prior.at[:, lanes], prior_send.at[k], prior_recv.at[k], next_t, s)
        )
        shift_copies[k].start()

    def greet_joined(i, carry):
        greet(joined, peer_yh(i), s)
        return carry

    lax.fori_loop(1, 8, greet_joined, 0)
    base = pl.multiple_of(jnp.minimum(lax.div(jnp.maximum(2 * q - 1, 0), 16), 14) * 128, 128)
    window = pl.ds(base, 256)
    edge_copies = []
    for k, ref in enumerate((d_hbm, wr_hbm, wc_hbm)):
        edge_copies.append(
            remote(ref.at[pl.ds(ROWS - 8, 8), window], edge_top.at[k], edge_send.at[k], edge_recv.at[k], t, down_s)
        )
        edge_copies.append(
            remote(ref.at[pl.ds(0, 8), window], edge_low.at[k], edge_send.at[3 + k], edge_recv.at[3 + k], t, up_s)
        )
    for copy in edge_copies:
        copy.start()

    for copy in loads:
        copy.wait()
    field = u_ref[...]
    row = lax.broadcasted_iota(jnp.int32, (ROWS, COLS), 0)
    col = lax.broadcasted_iota(jnp.int32, (ROWS, COLS), 1)
    row_prior = jnp.where(row == 0, 0.0, pltpu.roll(field, 1, axis=0))
    row_next = jnp.where(row == ROWS - 1, 0.0, pltpu.roll(field, ROWS - 1, axis=0))
    col_prior = jnp.where(col == 0, 0.0, pltpu.roll(field, 1, axis=1))
    col_next = jnp.where(col == COLS - 1, 0.0, pltpu.roll(field, COLS - 1, axis=1))
    image = (
        field
        + d_ref[...] * (4.0 * field - row_next - row_prior - col_next - col_prior)
        + 0.5 * wr_ref[...] * (row_next - row_prior)
        + 0.5 * wc_ref[...] * (col_next - col_prior)
    )
    plain[...] = rs_ref[...] - image
    for copy in row_copies:
        copy.wait()
    top = jnp.where(s > 0, above[...], 0.0)
    low = jnp.where(s < 3, below[...], 0.0)
    plain[0:1, :] += (d_ref[0:1, :] + 0.5 * wr_ref[0:1, :]) * top
    plain[ROWS - 1 : ROWS, :] += (d_ref[ROWS - 1 : ROWS, :] - 0.5 * wr_ref[ROWS - 1 : ROWS, :]) * low

    for k in range(4):
        shift_copies[k].wait()
        part = part_of(t, k)

        def pack(i, carry):
            cb = part * 4 + i
            lanes = pl.ds(pl.multiple_of(cb * 128, 128), 128)
            residual = plain[:, lanes] + jnp.where(t > 0, prior[:, lanes], 0.0)
            sent[:, pl.ds(pl.multiple_of(cb * 8, 8), 8), :] = swap_groups(residual.reshape(4, 8, 128))
            return carry

        def send_stripe(i, carry):
            stripe = part * 32 + lax.rem(y + 1 + i, 2) * 16 + lax.rem(z + far(lax.div(i, 2)), 16)
            remote(
                sent.at[:, pl.ds(stripe, 1), :], got.at[:, pl.ds(t, 1), :], out_send.at[0], out_recv.at[0],
                holder_of(stripe), s,
            ).start()
            return carry

        lax.fori_loop(0, 4, pack, 0, unroll=True)
        if k == 0:
            pl.semaphore_wait(joined, 7)
        lax.fori_loop(0, 31 if k == 0 else 32, send_stripe, 0)
    own = pltpu.make_async_copy(sent.at[:, pl.ds(q, 1), :], got.at[:, pl.ds(t, 1), :], own_sem)
    own.start()

    for copy in edge_copies:
        copy.wait()
    stack[...] = jnp.zeros_like(stack)
    for k, ref in enumerate((d_ref, wr_ref, wc_ref)):
        stack[pl.ds(38 * k, 3), :] = edge_top[k, 5:8, :]
        stack[pl.ds(38 * k + 3, ROWS), :] = ref[:, window]
        stack[pl.ds(38 * k + 35, 3), :] = edge_low[k, 0:3, :]
    turned[0:8, :] = jnp.zeros((8, 128), jnp.float32)
    turned[264:272, :] = jnp.zeros((8, 128), jnp.float32)
    turned[8:136, :] = stack[:, 0:128].T
    turned[136:264, :] = stack[:, 128:256].T
    offset = 16 * q - base
    left_tile = turned[pl.ds(pl.multiple_of(offset, 8), 8), :]
    middle = turned[pl.ds(pl.multiple_of(offset + 8, 8), 16), :]
    right_tile = turned[pl.ds(pl.multiple_of(offset + 24, 8), 8), :]
    tile_row = lax.broadcasted_iota(jnp.int32, (8, 128), 0)
    columns = jnp.concatenate([middle, jnp.where(tile_row < 4, right_tile, left_tile)], axis=0)
    cell = lax.broadcasted_iota(jnp.int32, (24, 128), 0)
    inside_cols = jnp.logical_and(
        jnp.logical_or(cell < 16, jnp.logical_or(cell >= 20, q < T - 1)), jnp.logical_or(cell < 20, q > 0)
    )
    shift_re = shift_ref[0:1, :]
    shift_im = shift_ref[1:2, :]

    def prepare(r, carry):
        def spread(k):
            turn = lax.rem(256 - 38 * k - r, 128)
            return jnp.broadcast_to(pltpu.roll(columns, turn, axis=1)[:, 0:1], (24, 128))

        diffusion = spread(0)
        half_rows = 0.5 * spread(1)
        half_cols = 0.5 * spread(2)
        south[r] = diffusion - half_rows
        north[r] = diffusion + half_rows
        east[r] = diffusion - half_cols
        west[r] = diffusion + half_cols
        diag = 1.0 - shift_re + 4.0 * diffusion
        modulus = 1.0 / (diag * diag + shift_im * shift_im)
        grid_row = s * ROWS + r - 3
        inside = jnp.logical_and(inside_cols, jnp.logical_and(grid_row >= 0, grid_row < 128))
        inv_a[r] = jnp.where(inside, diag * modulus, 0.0)
        inv_b[r] = jnp.where(inside, shift_im * modulus, 0.0)
        return carry

    lax.fori_loop(0, 38, prepare, 0, unroll=2)

    own.wait()
    arrived = remote(dummy, dummy, out_send.at[0], out_recv.at[0], next_t, s)
    arrived.wait_recv()
    for j in range(4):
        spectrum = product(split(got[j].T), split(fwd_ref[...]), ((1,), (0,)))
        src[pl.ds(3 + 8 * j, 8), 0:16, :] = spectrum.reshape(8, 16, 128)

    halo_copies = []
    for ds, at in ((-1, up_s), (0, s), (1, down_s)):
        from_row, to_row, rows = {-1: (3, 35, 3), 0: (3, 3, ROWS), 1: (ROWS, 0, 3)}[ds]
        for dq, who in ((-1, left_t), (0, t), (1, right_t)):
            if ds == 0 and dq == 0:
                continue
            from_col, to_col, cols = {-1: (0, 16, 4), 0: (0, 0, 16), 1: (12, 20, 4)}[dq]
            k = len(halo_copies)
            halo_copies.append(
                remote(
                    src.at[pl.ds(from_row, rows), pl.ds(from_col, cols), :],
                    src.at[pl.ds(to_row, rows), pl.ds(to_col, cols), :],
                    halo_send.at[k], halo_recv.at[k], who, at,
                )
            )
    for copy in halo_copies:
        copy.start()

    def times_inverse(v, cells):
        return v * inv_a[cells] + pltpu.roll(v, 64, axis=2) * inv_b[cells]

    def first(*cells):
        est_a[cells] = RELAX_WEIGHTS[0] * times_inverse(src[cells], cells)

    for r in range(3, 35):
        first(pl.ds(r, 1), pl.ds(0, 16))
    arrived.wait_send()
    for copy in halo_copies:
        copy.wait()
    for r in (0, 1, 2, 35, 36, 37):
        first(pl.ds(r, 1))
    for r in range(3, 35):
        first(pl.ds(r, 1), pl.ds(16, 8))

    def sweep(weight, start, count, old, new):
        def step(i, carry):
            begin = start + count * i
            rows = pl.ds(begin, count)
            here = old[rows]
            near = (
                south[rows] * old[pl.ds(begin + 1, count)]
                + north[rows] * old[pl.ds(begin - 1, count)]
                + east[rows] * pltpu.roll(here, 23, axis=1)
                + west[rows] * pltpu.roll(here, 1, axis=1)
            )
            moved = times_inverse(src[rows] + near, (rows,))
            new[rows] = (1.0 - weight) * here + weight * moved
            return carry

        return step

    lax.fori_loop(0, 18, sweep(RELAX_WEIGHTS[1], 1, 2, est_a, est_b), 0, unroll=6)
    lax.fori_loop(0, 17, sweep(RELAX_WEIGHTS[2], 2, 2, est_b, est_a), 0, unroll=17)
    lax.fori_loop(0, 16, sweep(RELAX_WEIGHTS[3], 3, 2, est_a, est_b), 0, unroll=8)

    for j in range(4):
        estimate = est_b[pl.ds(3 + 8 * j, 8), 0:16, :].reshape(128, 128)
        made[j] = product(split(back_ref[...]), split(estimate), ((1,), (1,)))

    def send_step(i, carry):
        who = peer(i)
        remote(
            made.at[:, pl.ds(who, 1), :], back_got.at[:, pl.ds(q, 1), :], out_send.at[1], out_recv.at[1], who, s
        ).start()
        return carry

    lax.fori_loop(0, T - 1, send_step, 0)
    own_back = pltpu.make_async_copy(made.at[:, pl.ds(t, 1), :], back_got.at[:, pl.ds(q, 1), :], own_sem)
    own_back.start()
    own_back.wait()
    returned = remote(dummy, dummy, out_send.at[1], out_recv.at[1], next_t, s)
    returned.wait()

    def unpack(cb, carry):
        lanes = pl.ds(pl.multiple_of(cb * 128, 128), 128)
        restored = swap_groups(back_got[:, pl.ds(pl.multiple_of(cb * 8, 8), 8), :])
        out_ref[0, :, lanes] = u_ref[:, lanes] + restored.reshape(ROWS, 128)
        return carry

    lax.fori_loop(0, 16, unpack, 0, unroll=8)


def shards(right_side, iterate, diffusion, wind_rows, wind_cols):
    forward, back, shift = (jnp.asarray(a) for a in tables())
    vmem = pl.BlockSpec(memory_space=pltpu.VMEM)
    dma = pltpu.SemaphoreType.DMA

    def space(*shape):
        return pltpu.VMEM(shape, jnp.float32)

    scratch = [space(ROWS, COLS)] * 5 + [space(T, T), space(T, T), space(8, T)]
    scratch += [
        space(1, COLS), space(1, COLS), space(ROWS, COLS),
        space(3, 8, 256), space(3, 8, 256),
        space(ROWS, COLS), space(4, T, 128), space(4, T, 128),
        space(4, T, 128), space(4, T, 128),
        space(128, 256), space(272, 128),
    ]
    scratch += [space(38, 24, 128)] * 9
    scratch += [space(T - 1, 4, 128)]
    scratch += [
        dma((2,)), dma((2,)), dma((4,)), dma((4,)), dma((6,)), dma((6,)), dma((8,)), dma((8,)), dma((2,)), dma((2,)), dma, dma((8,)),
        pltpu.SemaphoreType.REGULAR,
    ]
    return pl.pallas_call(
        kernel,
        out_shape=pltpu.VMEM(iterate.shape, jnp.float32),
        in_specs=[pl.BlockSpec(memory_space=pltpu.HBM)] * 8,
        out_specs=vmem,
        scratch_shapes=scratch,
        compiler_params=pltpu.CompilerParams(
            collective_id=0, has_side_effects=True, vmem_limit_bytes=60 * 1024 * 1024
        ),
        name="correction",
    )(right_side, iterate, diffusion, wind_rows, wind_cols, forward, back, shift)


def solution(mesh):
    fields = P("tm", "space", None)
    cells = P("space", None)
    return jax.shard_map(
        shards, mesh=mesh, in_specs=(fields, fields, cells, cells, cells), out_specs=fields, check_vma=False
    )
```

```python
import math

import jax
import jax.numpy as jnp
import numpy as np
from jax import lax
from jax.experimental import pallas as pl
from jax.experimental.pallas import tpu as pltpu
from jax.sharding import PartitionSpec as P

MESH = pl.DeviceIdType.MESH
ALPHA = 0.1
RELAX_WEIGHTS = (0.7, 0.9, 0.8, 1.0)
T = 128
ROWS = 32
COLS = 2048


def tables():
    n = np.arange(T)
    k = np.arange(64)
    rate = math.log(ALPHA) / T
    angle = 2.0 * math.pi * ((n[:, None] * k[None, :]) % T) / T
    forward = np.concatenate([np.cos(angle), -np.sin(angle)], axis=1)
    forward[:, 64] = np.where(n % 2 == 0, 1.0, -1.0)
    back = 2.0 * forward
    back[:, 0] *= 0.5
    back[:, 64] *= 0.5
    forward = forward * np.exp(n * rate)[:, None]
    back = back * (np.exp(-n * rate) / T)[:, None]
    radius = math.exp(rate)
    phase = 2.0 * math.pi * k / T
    shift = np.zeros((8, T))
    shift[0, :64] = radius * np.cos(phase)
    shift[0, 64:] = radius * np.cos(phase)
    shift[0, 64] = -radius
    shift[1, :64] = radius * np.sin(phase)
    shift[1, 64:] = -radius * np.sin(phase)
    shift[1, 64] = 0.0
    return [np.asarray(a, np.float32) for a in (forward, back, shift)]


def stripe_of(t):
    return lax.rem(t, 2) * 64 + lax.div(t, 32) * 16 + lax.rem(lax.div(t, 2), 16)


def holder_of(q):
    return lax.rem(lax.div(q, 16), 4) * 32 + lax.rem(q, 16) * 2 + lax.div(q, 64)


def split(v):
    high = v.astype(jnp.bfloat16)
    return high, (v - high.astype(jnp.float32)).astype(jnp.bfloat16)


def product(a, b, dims):
    terms = [
        lax.dot_general(left, right, (dims, ((), ())), preferred_element_type=jnp.float32)
        for left, right in ((a[0], b[0]), (a[0], b[1]), (a[1], b[0]))
    ]
    return terms[0] + (terms[1] + terms[2])


def swap_groups(v):
    row = lax.broadcasted_iota(jnp.int32, v.shape, 1)
    lane = lax.broadcasted_iota(jnp.int32, v.shape, 2)
    for m in (1, 2, 4):
        low_row = row & m == 0
        low_lane = lane & (16 * m) == 0
        up = pltpu.roll(pltpu.roll(v, 8 - m, axis=1), 16 * m, axis=2)
        down = up if m == 4 else pltpu.roll(pltpu.roll(v, m, axis=1), 128 - 16 * m, axis=2)
        v = jnp.where(low_row == low_lane, v, jnp.where(low_row, up, down))
    return v


def kernel(
    rs_hbm, u_hbm, d_hbm, wr_hbm, wc_hbm, fwd_hbm, back_hbm, shift_hbm, out_ref,
    rs_ref, u_ref, d_ref, wr_ref, wc_ref, fwd_ref, back_ref, shift_ref,
    above, below, prior, edge_top, edge_low, plain, sent, got, made, back_got, stack, turned,
    north, south, east, west, inv_a, inv_b, src, est_a, est_b, dummy,
    row_send, row_recv, prior_send, prior_recv, edge_send, edge_recv,
    halo_send, halo_recv, out_send, out_recv, own_sem, load_sem, joined,
):
    loads = []
    for k, (source, target) in enumerate(
        (
            (u_hbm.at[0], u_ref), (d_hbm, d_ref), (wr_hbm, wr_ref), (wc_hbm, wc_ref), (rs_hbm.at[0], rs_ref),
            (fwd_hbm, fwd_ref), (back_hbm, back_ref), (shift_hbm, shift_ref),
        )
    ):
        loads.append(pltpu.make_async_copy(source, target, load_sem.at[k]))
        loads[k].start()
    t = lax.axis_index("tm")
    s = lax.axis_index("space")
    y, z, h = lax.div(t, 32), lax.rem(lax.div(t, 2), 16), lax.rem(t, 2)
    q = stripe_of(t)
    up_s, down_s = lax.rem(s + 3, 4), lax.rem(s + 1, 4)
    next_t, prior_t = lax.rem(t + 1, T), lax.rem(t + T - 1, T)
    left_t, right_t = holder_of(lax.rem(q + T - 1, T)), holder_of(lax.rem(q + 1, T))

    def peer_z(i):
        return y * 32 + lax.rem(z + i, 16) * 2 + h

    def peer_yh(i):
        g = lax.rem(y * 2 + h + i, 8)
        return lax.div(g, 2) * 32 + z * 2 + lax.rem(g, 2)

    def far(i):
        half = lax.div(16 - i, 2)
        return lax.rem(lax.rem(15 - i, 2) * 2 * half - half + 16, 16)

    def peer(i):
        g = lax.rem(y * 2 + h + 7 - lax.rem(i, 8), 8)
        return lax.div(g, 2) * 32 + lax.rem(z + far(lax.div(i, 8)), 16) * 2 + lax.rem(g, 2)

    def part_of(who, k):
        return lax.rem(lax.div(stripe_of(who), 32) + 4 - k, 4)

    def part_lanes(who, k):
        return pl.ds(pl.multiple_of(part_of(who, k) * 512, 512), 512)

    barrier = pltpu.get_barrier_semaphore()

    def greet(semaphore, who, at):
        pl.semaphore_signal(semaphore, inc=1, device_id=(who, at), device_id_type=MESH)

    def greet_z(i, carry):
        greet(barrier, peer_z(i), s)
        return carry

    def greet_yh(i, carry):
        greet(barrier, peer_yh(i), s)
        return carry

    for at in (up_s, down_s):
        for who in (t, left_t, right_t):
            greet(barrier, who, at)
    for who in (next_t, prior_t, left_t, right_t):
        greet(barrier, who, s)
    lax.fori_loop(1, 16, greet_z, 0)
    lax.fori_loop(1, 8, greet_yh, 0)
    pl.semaphore_wait(barrier, 32)

    def remote(source, target, send, recv, who, at):
        return pltpu.make_async_remote_copy(
            src_ref=source, dst_ref=target, send_sem=send, recv_sem=recv,
            device_id=(who, at), device_id_type=MESH,
        )

    row_copies = [
        remote(u_hbm.at[0, pl.ds(ROWS - 1, 1)], above, row_send.at[0], row_recv.at[0], t, down_s),
        remote(u_hbm.at[0, pl.ds(0, 1)], below, row_send.at[1], row_recv.at[1], t, up_s),
    ]
    for copy in row_copies:
        copy.start()
    shift_copies = []
    for k in range(4):
        lanes = part_lanes(next_t, k)
        shift_copies.append(
            remote(u_hbm.at[0, :, lanes], prior.at[:, lanes], prior_send.at[k], prior_recv.at[k], next_t, s)
        )
        shift_copies[k].start()

    def greet_joined(i, carry):
        greet(joined, peer_yh(i), s)
        return carry

    lax.fori_loop(1, 8, greet_joined, 0)
    base = pl.multiple_of(jnp.minimum(lax.div(jnp.maximum(2 * q - 1, 0), 16), 14) * 128, 128)
    window = pl.ds(base, 256)
    edge_copies = []
    for k, ref in enumerate((d_hbm, wr_hbm, wc_hbm)):
        edge_copies.append(
            remote(ref.at[pl.ds(ROWS - 8, 8), window], edge_top.at[k], edge_send.at[k], edge_recv.at[k], t, down_s)
        )
        edge_copies.append(
            remote(ref.at[pl.ds(0, 8), window], edge_low.at[k], edge_send.at[3 + k], edge_recv.at[3 + k], t, up_s)
        )
    for copy in edge_copies:
        copy.start()

    for copy in loads:
        copy.wait()
    field = u_ref[...]
    row = lax.broadcasted_iota(jnp.int32, (ROWS, COLS), 0)
    col = lax.broadcasted_iota(jnp.int32, (ROWS, COLS), 1)
    row_prior = jnp.where(row == 0, 0.0, pltpu.roll(field, 1, axis=0))
    row_next = jnp.where(row == ROWS - 1, 0.0, pltpu.roll(field, ROWS - 1, axis=0))
    col_prior = jnp.where(col == 0, 0.0, pltpu.roll(field, 1, axis=1))
    col_next = jnp.where(col == COLS - 1, 0.0, pltpu.roll(field, COLS - 1, axis=1))
    image = (
        field
        + d_ref[...] * (4.0 * field - row_next - row_prior - col_next - col_prior)
        + 0.5 * wr_ref[...] * (row_next - row_prior)
        + 0.5 * wc_ref[...] * (col_next - col_prior)
    )
    plain[...] = rs_ref[...] - image
    for copy in row_copies:
        copy.wait()
    top = jnp.where(s > 0, above[...], 0.0)
    low = jnp.where(s < 3, below[...], 0.0)
    plain[0:1, :] += (d_ref[0:1, :] + 0.5 * wr_ref[0:1, :]) * top
    plain[ROWS - 1 : ROWS, :] += (d_ref[ROWS - 1 : ROWS, :] - 0.5 * wr_ref[ROWS - 1 : ROWS, :]) * low

    for k in range(4):
        shift_copies[k].wait()
        part = part_of(t, k)

        def pack(i, carry):
            cb = part * 4 + i
            lanes = pl.ds(pl.multiple_of(cb * 128, 128), 128)
            residual = plain[:, lanes] + jnp.where(t > 0, prior[:, lanes], 0.0)
            sent[:, pl.ds(pl.multiple_of(cb * 8, 8), 8), :] = swap_groups(residual.reshape(4, 8, 128))
            return carry

        def send_stripe(i, carry):
            stripe = part * 32 + lax.rem(y + 1 + i, 2) * 16 + lax.rem(z + far(lax.div(i, 2)), 16)
            remote(
                sent.at[:, pl.ds(stripe, 1), :], got.at[:, pl.ds(t, 1), :], out_send.at[0], out_recv.at[0],
                holder_of(stripe), s,
            ).start()
            return carry

        lax.fori_loop(0, 4, pack, 0, unroll=True)
        if k == 0:
            pl.semaphore_wait(joined, 7)
        lax.fori_loop(0, 31 if k == 0 else 32, send_stripe, 0, unroll=4)
    own = pltpu.make_async_copy(sent.at[:, pl.ds(q, 1), :], got.at[:, pl.ds(t, 1), :], own_sem)
    own.start()

    for copy in edge_copies:
        copy.wait()
    stack[...] = jnp.zeros_like(stack)
    for k, ref in enumerate((d_ref, wr_ref, wc_ref)):
        stack[pl.ds(38 * k, 3), :] = edge_top[k, 5:8, :]
        stack[pl.ds(38 * k + 3, ROWS), :] = ref[:, window]
        stack[pl.ds(38 * k + 35, 3), :] = edge_low[k, 0:3, :]
    turned[0:8, :] = jnp.zeros((8, 128), jnp.float32)
    turned[264:272, :] = jnp.zeros((8, 128), jnp.float32)
    turned[8:136, :] = stack[:, 0:128].T
    turned[136:264, :] = stack[:, 128:256].T
    offset = 16 * q - base
    left_tile = turned[pl.ds(pl.multiple_of(offset, 8), 8), :]
    middle = turned[pl.ds(pl.multiple_of(offset + 8, 8), 16), :]
    right_tile = turned[pl.ds(pl.multiple_of(offset + 24, 8), 8), :]
    tile_row = lax.broadcasted_iota(jnp.int32, (8, 128), 0)
    columns = jnp.concatenate([middle, jnp.where(tile_row < 4, right_tile, left_tile)], axis=0)
    cell = lax.broadcasted_iota(jnp.int32, (24, 128), 0)
    inside_cols = jnp.logical_and(
        jnp.logical_or(cell < 16, jnp.logical_or(cell >= 20, q < T - 1)), jnp.logical_or(cell < 20, q > 0)
    )
    shift_re = shift_ref[0:1, :]
    shift_im = shift_ref[1:2, :]

    def prepare(r, carry):
        def spread(k):
            turn = lax.rem(256 - 38 * k - r, 128)
            return jnp.broadcast_to(pltpu.roll(columns, turn, axis=1)[:, 0:1], (24, 128))

        diffusion = spread(0)
        half_rows = 0.5 * spread(1)
        half_cols = 0.5 * spread(2)
        south[r] = diffusion - half_rows
        north[r] = diffusion + half_rows
        east[r] = diffusion - half_cols
        west[r] = diffusion + half_cols
        diag = 1.0 - shift_re + 4.0 * diffusion
        modulus = 1.0 / (diag * diag + shift_im * shift_im)
        grid_row = s * ROWS + r - 3
        inside = jnp.logical_and(inside_cols, jnp.logical_and(grid_row >= 0, grid_row < 128))
        inv_a[r] = jnp.where(inside, diag * modulus, 0.0)
        inv_b[r] = jnp.where(inside, shift_im * modulus, 0.0)
        return carry

    lax.fori_loop(0, 38, prepare, 0, unroll=2)

    own.wait()
    arrived = remote(dummy, dummy, out_send.at[0], out_recv.at[0], next_t, s)
    arrived.wait_recv()
    halo_copies = []

    def give(from_row, to_row, rows, side, who, at):
        from_col, to_col, cols = ((0, 16, 4), (0, 0, 16), (12, 20, 4))[side]
        k = len(halo_copies)
        halo_copies.append(
            remote(
                src.at[pl.ds(from_row, rows), pl.ds(from_col, cols), :],
                src.at[pl.ds(to_row, rows), pl.ds(to_col, cols), :],
                halo_send.at[k], halo_recv.at[k], who, at,
            )
        )
        halo_copies[k].start()

    forward = split(fwd_ref[...])
    for j in (0, 3, 1, 2):
        spectrum = product(split(got[j].T), forward, ((1,), (0,)))
        begin = 3 + 8 * j
        src[pl.ds(begin, 8), 0:16, :] = spectrum.reshape(8, 16, 128)
        for side, who in ((0, left_t), (2, right_t)):
            give(begin, begin, 8, side, who, s)
        if j in (0, 3):
            from_row, to_row, at = (3, 35, up_s) if j == 0 else (ROWS, 0, down_s)
            for side, who in enumerate((left_t, t, right_t)):
                give(from_row, to_row, 3, side, who, at)

    def times_inverse(v, cells):
        return v * inv_a[cells] + pltpu.roll(v, 64, axis=2) * inv_b[cells]

    def first(*cells):
        est_a[cells] = RELAX_WEIGHTS[0] * times_inverse(src[cells], cells)

    for r in range(3, 35):
        first(pl.ds(r, 1), pl.ds(0, 16))
    arrived.wait_send()
    for copy in halo_copies:
        copy.wait()
    for r in (0, 1, 2, 35, 36, 37):
        first(pl.ds(r, 1))
    for r in range(3, 35):
        first(pl.ds(r, 1), pl.ds(16, 8))

    def sweep(weight, start, count, old, new):
        def step(i, carry):
            begin = start + count * i
            rows = pl.ds(begin, count)
            here = old[rows]
            near = (
                south[rows] * old[pl.ds(begin + 1, count)]
                + north[rows] * old[pl.ds(begin - 1, count)]
                + east[rows] * pltpu.roll(here, 23, axis=1)
                + west[rows] * pltpu.roll(here, 1, axis=1)
            )
            moved = times_inverse(src[rows] + near, (rows,))
            new[rows] = (1.0 - weight) * here + weight * moved
            return carry

        return step

    lax.fori_loop(0, 18, sweep(RELAX_WEIGHTS[1], 1, 2, est_a, est_b), 0, unroll=6)
    lax.fori_loop(0, 17, sweep(RELAX_WEIGHTS[2], 2, 2, est_b, est_a), 0, unroll=17)
    backward = split(back_ref[...])
    last = sweep(RELAX_WEIGHTS[3], 3, 2, est_a, est_b)
    for j in range(4):
        for i in range(4 * j, 4 * j + 4):
            last(i, 0)
        estimate = est_b[pl.ds(3 + 8 * j, 8), 0:16, :].reshape(128, 128)
        made[j] = product(backward, split(estimate), ((1,), (1,)))

    def send_step(i, carry):
        who = peer(i)
        remote(
            made.at[:, pl.ds(who, 1), :], back_got.at[:, pl.ds(q, 1), :], out_send.at[1], out_recv.at[1], who, s
        ).start()
        return carry

    lax.fori_loop(0, T - 1, send_step, 0, unroll=4)
    own_back = pltpu.make_async_copy(made.at[:, pl.ds(t, 1), :], back_got.at[:, pl.ds(q, 1), :], own_sem)
    own_back.start()
    own_back.wait()
    returned = remote(dummy, dummy, out_send.at[1], out_recv.at[1], next_t, s)
    returned.wait()

    def unpack(cb, carry):
        lanes = pl.ds(pl.multiple_of(cb * 128, 128), 128)
        restored = swap_groups(back_got[:, pl.ds(pl.multiple_of(cb * 8, 8), 8), :])
        out_ref[0, :, lanes] = u_ref[:, lanes] + restored.reshape(ROWS, 128)
        return carry

    lax.fori_loop(0, 16, unpack, 0, unroll=8)


def shards(right_side, iterate, diffusion, wind_rows, wind_cols):
    forward, back, shift = (jnp.asarray(a) for a in tables())
    vmem = pl.BlockSpec(memory_space=pltpu.VMEM)
    dma = pltpu.SemaphoreType.DMA

    def space(*shape):
        return pltpu.VMEM(shape, jnp.float32)

    scratch = [space(ROWS, COLS)] * 5 + [space(T, T), space(T, T), space(8, T)]
    scratch += [
        space(1, COLS), space(1, COLS), space(ROWS, COLS),
        space(3, 8, 256), space(3, 8, 256),
        space(ROWS, COLS), space(4, T, 128), space(4, T, 128),
        space(4, T, 128), space(4, T, 128),
        space(128, 256), space(272, 128),
    ]
    scratch += [space(38, 24, 128)] * 9
    scratch += [space(T - 1, 4, 128)]
    scratch += [
        dma((2,)), dma((2,)), dma((4,)), dma((4,)), dma((6,)), dma((6,)), dma((14,)), dma((14,)), dma((2,)), dma((2,)), dma, dma((8,)),
        pltpu.SemaphoreType.REGULAR,
    ]
    return pl.pallas_call(
        kernel,
        out_shape=pltpu.VMEM(iterate.shape, jnp.float32),
        in_specs=[pl.BlockSpec(memory_space=pltpu.HBM)] * 8,
        out_specs=vmem,
        scratch_shapes=scratch,
        compiler_params=pltpu.CompilerParams(
            collective_id=0, has_side_effects=True, vmem_limit_bytes=60 * 1024 * 1024
        ),
        name="correction",
    )(right_side, iterate, diffusion, wind_rows, wind_cols, forward, back, shift)


def solution(mesh):
    fields = P("tm", "space", None)
    cells = P("space", None)
    return jax.shard_map(
        shards, mesh=mesh, in_specs=(fields, fields, cells, cells, cells), out_specs=fields, check_vma=False
    )
```

```python
import math

import jax
import jax.numpy as jnp
import numpy as np
from jax import lax
from jax.experimental import pallas as pl
from jax.experimental.pallas import tpu as pltpu
from jax.sharding import PartitionSpec as P

MESH = pl.DeviceIdType.MESH
ALPHA = 0.1
RELAX_WEIGHTS = (0.7, 0.9, 0.8, 1.0)
T = 128
ROWS = 32
COLS = 2048


def tables():
    n = np.arange(T)
    k = np.arange(64)
    rate = math.log(ALPHA) / T
    angle = 2.0 * math.pi * ((n[:, None] * k[None, :]) % T) / T
    forward = np.concatenate([np.cos(angle), -np.sin(angle)], axis=1)
    forward[:, 64] = np.where(n % 2 == 0, 1.0, -1.0)
    back = 2.0 * forward
    back[:, 0] *= 0.5
    back[:, 64] *= 0.5
    forward = forward * np.exp(n * rate)[:, None]
    back = back * (np.exp(-n * rate) / T)[:, None]
    radius = math.exp(rate)
    phase = 2.0 * math.pi * k / T
    shift = np.zeros((8, T))
    shift[0, :64] = radius * np.cos(phase)
    shift[0, 64:] = radius * np.cos(phase)
    shift[0, 64] = -radius
    shift[1, :64] = radius * np.sin(phase)
    shift[1, 64:] = -radius * np.sin(phase)
    shift[1, 64] = 0.0
    return [np.asarray(a, np.float32) for a in (forward, back, shift)]


def stripe_of(t):
    return lax.rem(t, 2) * 64 + lax.div(t, 32) * 16 + lax.rem(lax.div(t, 2), 16)


def holder_of(q):
    return lax.rem(lax.div(q, 16), 4) * 32 + lax.rem(q, 16) * 2 + lax.div(q, 64)


def split(v):
    high = v.astype(jnp.bfloat16)
    return high, (v - high.astype(jnp.float32)).astype(jnp.bfloat16)


def product(a, b, dims):
    terms = [
        lax.dot_general(left, right, (dims, ((), ())), preferred_element_type=jnp.float32)
        for left, right in ((a[0], b[0]), (a[0], b[1]), (a[1], b[0]))
    ]
    return terms[0] + (terms[1] + terms[2])


def swap_groups(v):
    row = lax.broadcasted_iota(jnp.int32, v.shape, 1)
    lane = lax.broadcasted_iota(jnp.int32, v.shape, 2)
    for m in (1, 2, 4):
        low_row = row & m == 0
        low_lane = lane & (16 * m) == 0
        up = pltpu.roll(pltpu.roll(v, 8 - m, axis=1), 16 * m, axis=2)
        down = up if m == 4 else pltpu.roll(pltpu.roll(v, m, axis=1), 128 - 16 * m, axis=2)
        v = jnp.where(low_row == low_lane, v, jnp.where(low_row, up, down))
    return v


def kernel(
    rs_hbm, u_hbm, d_hbm, wr_hbm, wc_hbm, fwd_hbm, back_hbm, shift_hbm, out_ref,
    rs_ref, u_ref, d_ref, wr_ref, wc_ref, fwd_ref, back_ref, shift_ref,
    above, below, prior, edge_top, edge_low, plain, sent, got, made, back_got, stack, turned,
    north, south, east, west, inv_a, inv_b, src, est_a, est_b, dummy,
    row_send, row_recv, prior_send, prior_recv, edge_send, edge_recv,
    halo_send, halo_recv, out_send, out_recv, own_sem, load_sem, joined,
):
    t = lax.axis_index("tm")
    s = lax.axis_index("space")
    y, z, h = lax.div(t, 32), lax.rem(lax.div(t, 2), 16), lax.rem(t, 2)
    q = stripe_of(t)
    up_s, down_s = lax.rem(s + 3, 4), lax.rem(s + 1, 4)
    next_t, prior_t = lax.rem(t + 1, T), lax.rem(t + T - 1, T)
    left_t, right_t = holder_of(lax.rem(q + T - 1, T)), holder_of(lax.rem(q + 1, T))

    def peer_z(i):
        return y * 32 + lax.rem(z + i, 16) * 2 + h

    def peer_yh(i):
        g = lax.rem(y * 2 + h + i, 8)
        return lax.div(g, 2) * 32 + z * 2 + lax.rem(g, 2)

    def far(i):
        half = lax.div(16 - i, 2)
        return lax.rem(lax.rem(15 - i, 2) * 2 * half - half + 16, 16)

    def peer(i):
        g = lax.rem(y * 2 + h + 7 - lax.rem(i, 8), 8)
        return lax.div(g, 2) * 32 + lax.rem(z + far(lax.div(i, 8)), 16) * 2 + lax.rem(g, 2)

    def part_of(who, k):
        return lax.rem(lax.div(stripe_of(who), 32) + 7 - k, 4)

    def part_lanes(who, k):
        return pl.ds(pl.multiple_of(part_of(who, k) * 512, 512), 512)

    barrier = pltpu.get_barrier_semaphore()

    def greet(semaphore, who, at):
        pl.semaphore_signal(semaphore, inc=1, device_id=(who, at), device_id_type=MESH)

    def greet_z(i, carry):
        greet(barrier, peer_z(i), s)
        return carry

    def greet_yh(i, carry):
        greet(barrier, peer_yh(i), s)
        return carry

    for at in (up_s, down_s):
        for who in (t, left_t, right_t):
            greet(barrier, who, at)
    for who in (next_t, prior_t, left_t, right_t):
        greet(barrier, who, s)
    lax.fori_loop(1, 16, greet_z, 0)
    lax.fori_loop(1, 8, greet_yh, 0)
    loads = []
    for k, (source, target) in enumerate(
        (
            (u_hbm.at[0], u_ref), (d_hbm, d_ref), (wr_hbm, wr_ref), (wc_hbm, wc_ref), (rs_hbm.at[0], rs_ref),
            (fwd_hbm, fwd_ref), (back_hbm, back_ref), (shift_hbm, shift_ref),
        )
    ):
        loads.append(pltpu.make_async_copy(source, target, load_sem.at[k]))
        loads[k].start()
    pl.semaphore_wait(barrier, 32)

    def remote(source, target, send, recv, who, at):
        return pltpu.make_async_remote_copy(
            src_ref=source, dst_ref=target, send_sem=send, recv_sem=recv,
            device_id=(who, at), device_id_type=MESH,
        )

    row_copies = [
        remote(u_hbm.at[0, pl.ds(ROWS - 1, 1)], above, row_send.at[0], row_recv.at[0], t, down_s),
        remote(u_hbm.at[0, pl.ds(0, 1)], below, row_send.at[1], row_recv.at[1], t, up_s),
    ]
    for copy in row_copies:
        copy.start()
    shift_copies = []
    for k in range(4):
        lanes = part_lanes(next_t, k)
        shift_copies.append(
            remote(u_hbm.at[0, :, lanes], prior.at[:, lanes], prior_send.at[k], prior_recv.at[k], next_t, s)
        )
        shift_copies[k].start()

    def greet_joined(i, carry):
        greet(joined, peer_yh(i), s)
        return carry

    lax.fori_loop(1, 8, greet_joined, 0)
    base = pl.multiple_of(jnp.minimum(lax.div(jnp.maximum(2 * q - 1, 0), 16), 14) * 128, 128)
    window = pl.ds(base, 256)
    edge_copies = []
    for k, ref in enumerate((d_hbm, wr_hbm, wc_hbm)):
        edge_copies.append(
            remote(ref.at[pl.ds(ROWS - 8, 8), window], edge_top.at[k], edge_send.at[k], edge_recv.at[k], t, down_s)
        )
        edge_copies.append(
            remote(ref.at[pl.ds(0, 8), window], edge_low.at[k], edge_send.at[3 + k], edge_recv.at[3 + k], t, up_s)
        )
    for copy in edge_copies:
        copy.start()

    for copy in loads:
        copy.wait()
    field = u_ref[...]
    row = lax.broadcasted_iota(jnp.int32, (ROWS, COLS), 0)
    col = lax.broadcasted_iota(jnp.int32, (ROWS, COLS), 1)
    row_prior = jnp.where(row == 0, 0.0, pltpu.roll(field, 1, axis=0))
    row_next = jnp.where(row == ROWS - 1, 0.0, pltpu.roll(field, ROWS - 1, axis=0))
    col_prior = jnp.where(col == 0, 0.0, pltpu.roll(field, 1, axis=1))
    col_next = jnp.where(col == COLS - 1, 0.0, pltpu.roll(field, COLS - 1, axis=1))
    image = (
        field
        + d_ref[...] * (4.0 * field - row_next - row_prior - col_next - col_prior)
        + 0.5 * wr_ref[...] * (row_next - row_prior)
        + 0.5 * wc_ref[...] * (col_next - col_prior)
    )
    plain[...] = rs_ref[...] - image
    for copy in row_copies:
        copy.wait()
    top = jnp.where(s > 0, above[...], 0.0)
    low = jnp.where(s < 3, below[...], 0.0)
    plain[0:1, :] += (d_ref[0:1, :] + 0.5 * wr_ref[0:1, :]) * top
    plain[ROWS - 1 : ROWS, :] += (d_ref[ROWS - 1 : ROWS, :] - 0.5 * wr_ref[ROWS - 1 : ROWS, :]) * low

    for k in range(4):
        shift_copies[k].wait()
        part = part_of(t, k)

        def pack(i, carry):
            cb = part * 4 + i
            lanes = pl.ds(pl.multiple_of(cb * 128, 128), 128)
            residual = plain[:, lanes] + jnp.where(t > 0, prior[:, lanes], 0.0)
            sent[:, pl.ds(pl.multiple_of(cb * 8, 8), 8), :] = swap_groups(residual.reshape(4, 8, 128))
            return carry

        def send_stripe(i, carry):
            stripe = part * 32 + lax.rem(y + 1 + i, 2) * 16 + lax.rem(z + far(lax.div(i, 2)), 16)
            remote(
                sent.at[:, pl.ds(stripe, 1), :], got.at[:, pl.ds(t, 1), :], out_send.at[0], out_recv.at[0],
                holder_of(stripe), s,
            ).start()
            return carry

        lax.fori_loop(0, 4, pack, 0, unroll=True)
        if k == 0:
            pl.semaphore_wait(joined, 7)
        lax.fori_loop(0, 31 if k == 3 else 32, send_stripe, 0, unroll=4)
    own = pltpu.make_async_copy(sent.at[:, pl.ds(q, 1), :], got.at[:, pl.ds(t, 1), :], own_sem)
    own.start()

    for copy in edge_copies:
        copy.wait()
    stack[...] = jnp.zeros_like(stack)
    for k, ref in enumerate((d_ref, wr_ref, wc_ref)):
        stack[pl.ds(38 * k, 3), :] = edge_top[k, 5:8, :]
        stack[pl.ds(38 * k + 3, ROWS), :] = ref[:, window]
        stack[pl.ds(38 * k + 35, 3), :] = edge_low[k, 0:3, :]
    turned[0:8, :] = jnp.zeros((8, 128), jnp.float32)
    turned[264:272, :] = jnp.zeros((8, 128), jnp.float32)
    turned[8:136, :] = stack[:, 0:128].T
    turned[136:264, :] = stack[:, 128:256].T
    offset = 16 * q - base
    left_tile = turned[pl.ds(pl.multiple_of(offset, 8), 8), :]
    middle = turned[pl.ds(pl.multiple_of(offset + 8, 8), 16), :]
    right_tile = turned[pl.ds(pl.multiple_of(offset + 24, 8), 8), :]
    tile_row = lax.broadcasted_iota(jnp.int32, (8, 128), 0)
    columns = jnp.concatenate([middle, jnp.where(tile_row < 4, right_tile, left_tile)], axis=0)
    cell = lax.broadcasted_iota(jnp.int32, (24, 128), 0)
    inside_cols = jnp.logical_and(
        jnp.logical_or(cell < 16, jnp.logical_or(cell >= 20, q < T - 1)), jnp.logical_or(cell < 20, q > 0)
    )
    shift_re = shift_ref[0:1, :]
    shift_im = shift_ref[1:2, :]

    def prepare(r, carry):
        def spread(k):
            turn = lax.rem(256 - 38 * k - r, 128)
            return jnp.broadcast_to(pltpu.roll(columns, turn, axis=1)[:, 0:1], (24, 128))

        diffusion = spread(0)
        half_rows = 0.5 * spread(1)
        half_cols = 0.5 * spread(2)
        south[r] = diffusion - half_rows
        north[r] = diffusion + half_rows
        east[r] = diffusion - half_cols
        west[r] = diffusion + half_cols
        diag = 1.0 - shift_re + 4.0 * diffusion
        modulus = 1.0 / (diag * diag + shift_im * shift_im)
        grid_row = s * ROWS + r - 3
        inside = jnp.logical_and(inside_cols, jnp.logical_and(grid_row >= 0, grid_row < 128))
        inv_a[r] = jnp.where(inside, diag * modulus, 0.0)
        inv_b[r] = jnp.where(inside, shift_im * modulus, 0.0)
        return carry

    lax.fori_loop(0, 38, prepare, 0, unroll=2)

    own.wait()
    arrived = remote(dummy, dummy, out_send.at[0], out_recv.at[0], next_t, s)
    arrived.wait_recv()
    halo_copies = []

    def give(from_row, to_row, rows, side, who, at):
        from_col, to_col, cols = ((0, 16, 4), (0, 0, 16), (12, 20, 4))[side]
        k = len(halo_copies)
        halo_copies.append(
            remote(
                src.at[pl.ds(from_row, rows), pl.ds(from_col, cols), :],
                src.at[pl.ds(to_row, rows), pl.ds(to_col, cols), :],
                halo_send.at[k], halo_recv.at[k], who, at,
            )
        )
        halo_copies[k].start()

    forward = split(fwd_ref[...])
    for j in (0, 3, 1, 2):
        spectrum = product(split(got[j].T), forward, ((1,), (0,)))
        begin = 3 + 8 * j
        src[pl.ds(begin, 8), 0:16, :] = spectrum.reshape(8, 16, 128)
        for side, who in ((0, left_t), (2, right_t)):
            give(begin, begin, 8, side, who, s)
        if j in (0, 3):
            from_row, to_row, at = (3, 35, up_s) if j == 0 else (ROWS, 0, down_s)
            for side, who in enumerate((left_t, t, right_t)):
                give(from_row, to_row, 3, side, who, at)

    def times_inverse(v, cells):
        return v * inv_a[cells] + pltpu.roll(v, 64, axis=2) * inv_b[cells]

    def first(*cells):
        est_a[cells] = RELAX_WEIGHTS[0] * times_inverse(src[cells], cells)

    for r in range(3, 35):
        first(pl.ds(r, 1), pl.ds(0, 16))
    arrived.wait_send()
    for copy in halo_copies:
        copy.wait()
    for r in (0, 1, 2, 35, 36, 37):
        first(pl.ds(r, 1))
    for r in range(3, 35):
        first(pl.ds(r, 1), pl.ds(16, 8))

    def sweep(weight, start, count, old, new):
        def step(i, carry):
            begin = start + count * i
            rows = pl.ds(begin, count)
            here = old[rows]
            near = (
                south[rows] * old[pl.ds(begin + 1, count)]
                + north[rows] * old[pl.ds(begin - 1, count)]
                + east[rows] * pltpu.roll(here, 23, axis=1)
                + west[rows] * pltpu.roll(here, 1, axis=1)
            )
            moved = times_inverse(src[rows] + near, (rows,))
            new[rows] = (1.0 - weight) * here + weight * moved
            return carry

        return step

    lax.fori_loop(0, 18, sweep(RELAX_WEIGHTS[1], 1, 2, est_a, est_b), 0, unroll=6)
    lax.fori_loop(0, 17, sweep(RELAX_WEIGHTS[2], 2, 2, est_b, est_a), 0, unroll=17)
    backward = split(back_ref[...])
    last = sweep(RELAX_WEIGHTS[3], 3, 2, est_a, est_b)
    for j in range(4):
        for i in range(4 * j, 4 * j + 4):
            last(i, 0)
        estimate = est_b[pl.ds(3 + 8 * j, 8), 0:16, :].reshape(128, 128)
        made[j] = product(backward, split(estimate), ((1,), (1,)))

    def send_step(i, carry):
        who = peer(i)
        remote(
            made.at[:, pl.ds(who, 1), :], back_got.at[:, pl.ds(q, 1), :], out_send.at[1], out_recv.at[1], who, s
        ).start()
        return carry

    lax.fori_loop(0, T - 1, send_step, 0, unroll=4)
    own_back = pltpu.make_async_copy(made.at[:, pl.ds(t, 1), :], back_got.at[:, pl.ds(q, 1), :], own_sem)
    own_back.start()
    own_back.wait()
    returned = remote(dummy, dummy, out_send.at[1], out_recv.at[1], next_t, s)
    returned.wait()

    def unpack(cb, carry):
        lanes = pl.ds(pl.multiple_of(cb * 128, 128), 128)
        restored = swap_groups(back_got[:, pl.ds(pl.multiple_of(cb * 8, 8), 8), :])
        out_ref[0, :, lanes] = u_ref[:, lanes] + restored.reshape(ROWS, 128)
        return carry

    lax.fori_loop(0, 16, unpack, 0, unroll=8)


def shards(right_side, iterate, diffusion, wind_rows, wind_cols):
    forward, back, shift = (jnp.asarray(a) for a in tables())
    vmem = pl.BlockSpec(memory_space=pltpu.VMEM)
    dma = pltpu.SemaphoreType.DMA

    def space(*shape):
        return pltpu.VMEM(shape, jnp.float32)

    scratch = [space(ROWS, COLS)] * 5 + [space(T, T), space(T, T), space(8, T)]
    scratch += [
        space(1, COLS), space(1, COLS), space(ROWS, COLS),
        space(3, 8, 256), space(3, 8, 256),
        space(ROWS, COLS), space(4, T, 128), space(4, T, 128),
        space(4, T, 128), space(4, T, 128),
        space(128, 256), space(272, 128),
    ]
    scratch += [space(38, 24, 128)] * 9
    scratch += [space(T - 1, 4, 128)]
    scratch += [
        dma((2,)), dma((2,)), dma((4,)), dma((4,)), dma((6,)), dma((6,)), dma((14,)), dma((14,)), dma((2,)), dma((2,)), dma, dma((8,)),
        pltpu.SemaphoreType.REGULAR,
    ]
    return pl.pallas_call(
        kernel,
        out_shape=pltpu.VMEM(iterate.shape, jnp.float32),
        in_specs=[pl.BlockSpec(memory_space=pltpu.HBM)] * 8,
        out_specs=vmem,
        scratch_shapes=scratch,
        compiler_params=pltpu.CompilerParams(
            collective_id=0, has_side_effects=True, vmem_limit_bytes=60 * 1024 * 1024
        ),
        name="correction",
    )(right_side, iterate, diffusion, wind_rows, wind_cols, forward, back, shift)


def solution(mesh):
    fields = P("tm", "space", None)
    cells = P("space", None)
    return jax.shard_map(
        shards, mesh=mesh, in_specs=(fields, fields, cells, cells, cells), out_specs=fields, check_vma=False
    )
```
